32 devices in a mesh: beam: 2 (over x), gx: 16 (over z, y, core).
Axes of the slice: x: 2, y: 2, z: 4, core: 2. Of those that a mesh axis runs over, the one named last changes fastest.
Arguments:
- filterbank: bfloat16 [4096, 2048], P(('beam', 'gx')), parts along dimension 0, may hold values from -61 to 61
- chan_delay: int32 [16, 2048], P(None, 'gx'), may hold values from 0 to 7
- sub_delay: int32 [1536, 64], replicated, may hold values from 0 to 15
- widths: int32 [1536], replicated, may hold values from 1 to 16
Outputs:
- snr: float32 [3072, 2048], P('beam', 'gx'), parts along dimension 0
The draws below stay inside these ranges and needn't reach their ends.
There are 2 independent parts, one for each index of `beam`. The reference program is written for one: setup_inputs(seed, part) draws one part's arguments, and reference() takes and returns one part's arrays. A program takes and returns all parts, laid end to end along the dimension named above; an argument that names none is the same for every part. Nothing has to cross between parts.
All inputs are finite; a program needn't handle non-finite values.
Results may differ from the reference program's by a relative error of at most 0.00059.
Values may be sent and summed in bfloat16 or wider, within the bound.
A program may use at most 128 MiB of HBM per device.

```python
import math
import jax
import jax.numpy as jnp
from jax import lax

SUBCH = 32
CHANS = 2048
NSUB = 64
SAMPLES = 2048
GROUPS = 16
PER_GROUP = 96
TRIALS = 1536
DELAY_ONE = 8
DELAY_TWO = 16
WMAX = 16


def draw_filterbank(key, part):
    base = jax.random.fold_in(key, 11)
    key_band, key_noise = jax.random.split(base, 2)
    time_ramp = 1.0 + 2.0 * jnp.arange(SAMPLES, dtype=jnp.float32) / (SAMPLES - 1)
    bandpass = jnp.exp(jax.random.uniform(key_band, (CHANS, 1), jnp.float32, math.log(0.5), math.log(2.0)))
    noise = jax.random.truncated_normal(key_noise, -6.0, 6.0, (CHANS, SAMPLES), jnp.float32)
    return (bandpass * time_ramp[None, :] * (noise + 0.05)).astype(jnp.bfloat16)


def place_ends(entries, stream_key, least, top_value):
    place = [jax.random.randint(jax.random.fold_in(stream_key, axis), (), 0, length) for axis, length in enumerate(entries.shape)]
    main_axis = entries.shape.index(max(entries.shape))
    neighbour = place[:main_axis] + [(place[main_axis] + 1) % entries.shape[main_axis]] + place[main_axis + 1:]
    return entries.at[tuple(place)].set(least).at[tuple(neighbour)].set(top_value)


def setup_inputs(seed: int = 0, part: int = 0) -> dict:
    key_of = jax.random.split(jax.random.key(seed), 5)
    part_keys = jax.random.split(jax.random.fold_in(key_of[4], part), 5)
    filterbank = draw_filterbank(jax.random.fold_in(jax.random.fold_in(key_of[4], part), 71), part)
    chan_delay = place_ends(jax.random.randint(key_of[1], (GROUPS, CHANS), 0, DELAY_ONE), jax.random.fold_in(key_of[1], 1), 0, DELAY_ONE - 1).astype(jnp.int32)
    sub_delay = place_ends(jax.random.randint(key_of[2], (TRIALS, NSUB), 0, DELAY_TWO), jax.random.fold_in(key_of[2], 1), 0, DELAY_TWO - 1).astype(jnp.int32)
    widths = place_ends(jax.random.randint(key_of[3], (TRIALS,), 1, WMAX + 1), jax.random.fold_in(key_of[3], 1), 1, WMAX).astype(jnp.int32)
    return dict(filterbank=filterbank, chan_delay=chan_delay, sub_delay=sub_delay, widths=widths)


def band_sum(inputs):
    band_rows, delay_rows = inputs

    def per_group(delay_line):
        return jax.vmap(lambda series_row, offset: lax.dynamic_slice_in_dim(series_row, offset, SAMPLES))(band_rows, delay_line)
    shifted = jax.vmap(per_group)(delay_rows)
    return lax.optimization_barrier(jnp.sum(shifted.astype(jnp.float32), axis=1)).astype(jnp.bfloat16)

def reference(filterbank, chan_delay, sub_delay, widths):
    padded = jnp.pad(filterbank, ((0, 0), (0, DELAY_ONE)))
    band_input = padded.reshape(NSUB, SUBCH, SAMPLES + DELAY_ONE)
    band_delays = jnp.transpose(chan_delay.reshape(GROUPS, NSUB, SUBCH), (1, 0, 2))
    subbands = lax.map(band_sum, (band_input, band_delays))
    subbands_pad = jnp.pad(subbands, ((0, 0), (0, 0), (0, DELAY_TWO)))

    def trial_series(inputs):
        trial_index, delay_line = inputs
        group_rows = lax.dynamic_index_in_dim(subbands_pad, trial_index // PER_GROUP, 1, keepdims=False)
        shifted = jax.vmap(lambda series_row, offset: lax.dynamic_slice_in_dim(series_row, offset, SAMPLES))(group_rows, delay_line)
        return lax.optimization_barrier(jnp.sum(shifted.astype(jnp.float32), axis=0))
    series = lax.map(trial_series, (jnp.arange(TRIALS, dtype=jnp.int32), sub_delay))
    average = lax.optimization_barrier(jnp.sum(series, axis=1)) / SAMPLES
    variance = lax.optimization_barrier(jnp.sum((series - average[:, None]) ** 2, axis=1)) / SAMPLES
    padded_series = jnp.pad(series, ((0, 0), (0, WMAX)))
    boxcar = jnp.zeros((TRIALS, SAMPLES), jnp.float32)
    for offset in range(WMAX):
        boxcar = boxcar + jnp.where(offset < widths[:, None], padded_series[:, offset:offset + SAMPLES], 0.0)
    width_float = widths.astype(jnp.float32)[:, None]
    return (boxcar - width_float * average[:, None]) / jnp.sqrt(width_float * (variance[:, None] + 1e-05))
```

```python
import functools
import jax
import jax.numpy as jnp
from jax import lax
from jax.experimental import pallas as pl
from jax.experimental.pallas import tpu as pltpu
from jax.sharding import PartitionSpec as P

SUBCH = 32
DELAY_ONE = 8
DELAY_TWO = 16
WMAX = 16
LANES = 128
ROWS = 16
PREBUILD_BYTES = 24 << 20
MESH = pl.DeviceIdType.MESH


def lane_index(rows):
    return lax.broadcasted_iota(jnp.int32, (rows, LANES), 1)


def shifted(here, after, offset):
    if offset == 0:
        return here
    mixed = jnp.where(lane_index(here.shape[0]) >= offset, here, after)
    return pltpu.roll(mixed, LANES - offset, 1)


def main_kernel(
    n,
    fb_ref,
    cd_ref,
    sd_ref,
    w_ref,
    box_ref,
    res_ref,
    send,
    recv,
    x_main,
    x_halo,
    lhs,
    parts,
    mine,
    result,
    final,
    send_sem,
    recv_sem,
    part_send,
    part_recv,
    final_send,
    final_recv,
):
    me = lax.axis_index("gx")
    groups = cd_ref.shape[0]
    bands_here = cd_ref.shape[1] // SUBCH
    trials, bands = sd_ref.shape
    per_group = trials // groups
    samples = fb_ref.shape[1]
    tiles = samples // LANES
    main_rows = bands_here * groups
    rep = max(1, LANES // bands)
    width_k = rep * bands
    steps = (DELAY_TWO + WMAX) // rep
    prebuilt = lhs.shape[0] == groups
    bf16, f32 = jnp.bfloat16, jnp.float32

    barrier = pltpu.get_barrier_semaphore()

    @pl.loop(1, n)
    def _(s):
        pl.semaphore_signal(
            barrier, inc=1, device_id={"gx": lax.rem(me + s, n)}, device_id_type=MESH
        )

    lane = lane_index(groups)
    delays = cd_ref[...]
    code = jnp.concatenate(
        [
            jnp.where((lane >= SUBCH * b) & (lane < SUBCH * (b + 1)), delays, -1)
            for b in range(bands_here)
        ],
        0,
    )
    choose = jnp.concatenate(
        [jnp.where(code == o, 1.0, 0.0).astype(bf16) for o in range(DELAY_ONE)], 1
    )

    def tile(j):
        return fb_ref[:, pl.ds(pl.multiple_of(j * LANES, LANES), LANES)]

    def put(j, block):
        send[j, 0:main_rows, :] = block.astype(bf16)
        packed = jnp.zeros((groups, LANES), f32)
        for b in range(bands_here):
            head = jnp.where(lane < 2 * ROWS, block[b * groups : (b + 1) * groups], 0.0)
            packed = packed + (head if b == 0 else pltpu.roll(head, 2 * ROWS * b, 1))
        send[lax.rem(j + n - 1, n), main_rows : main_rows + groups, :] = packed.astype(bf16)

    @pl.loop(0, tiles // 2)
    def _(pair):
        first, second = tile(2 * pair), tile(2 * pair + 1)
        third = tile(jnp.minimum(2 * pair + 2, tiles - 1))
        third = jnp.where(2 * pair + 2 < tiles, third, jnp.zeros_like(third))
        stacked = jnp.concatenate(
            [
                jnp.concatenate([shifted(first, second, o), shifted(second, third, o)], 1)
                for o in range(DELAY_ONE)
            ],
            0,
        )
        block = jnp.dot(choose, stacked, preferred_element_type=f32)
        put(2 * pair, block[:, :LANES])
        put(2 * pair + 1, block[:, LANES:])

    send[n - 1, main_rows : main_rows + groups, :] = jnp.zeros((groups, LANES), bf16)

    pl.semaphore_wait(barrier, n - 1)

    def slab_copy(s, source, target):
        return pltpu.make_async_remote_copy(
            src_ref=send.at[target],
            dst_ref=recv.at[source],
            send_sem=send_sem.at[s],
            recv_sem=recv_sem.at[source],
            device_id={"gx": target},
            device_id_type=MESH,
        )

    @pl.loop(1, n)
    def _(s):
        slab_copy(s, me, lax.rem(me + s, n)).start()

    recv[me] = send[me]

    def build(g, slot):
        rows = pl.ds(pl.multiple_of(g * per_group, per_group), per_group)
        own = sd_ref[rows, :]
        own = jnp.concatenate([own - h for h in range(rep)], 1)
        wide = w_ref[rows, :]
        if width_k > LANES:
            wide = jnp.concatenate([wide] * (width_k // LANES), 1)
        for p in range(steps):
            gap = p * rep - own
            columns = slice(p * width_k, (p + 1) * width_k)
            inside = jnp.where((gap >= 0) & (gap < wide), 1.0, 0.0)
            lhs[slot, 0:per_group, columns] = inside.astype(bf16)
            if p * rep < DELAY_TWO:
                lhs[slot, per_group : 2 * per_group, columns] = jnp.where(
                    gap == 0, 1.0, 0.0
                ).astype(bf16)

    if prebuilt:

        @pl.loop(0, groups)
        def _(g):
            build(g, g)

    own_rows = pl.ds(
        pl.multiple_of(jnp.minimum(me, groups - 1) * per_group, per_group), per_group
    )
    own_width = w_ref[own_rows, :].astype(f32).T[0:1, :]

    @pl.loop(1, n)
    def _(s):
        slab_copy(s, lax.rem(me + n - s, n), me).wait_recv()

    per_pack = ROWS // bands_here
    out_row = lax.broadcasted_iota(jnp.int32, (ROWS * groups, ROWS * groups), 0)
    in_row = lax.broadcasted_iota(jnp.int32, (ROWS * groups, ROWS * groups), 1)
    turn = jnp.where(
        in_row == (out_row & (ROWS - 1)) * groups + (out_row >> 4), 1.0, 0.0
    ).astype(bf16)

    @pl.loop(0, n // per_pack)
    def _(q):
        mains, halos = [], []
        for s in range(per_pack):
            mains.append(recv[q * per_pack + s, 0:main_rows, :])
            halo = recv[q * per_pack + s, main_rows : main_rows + groups, :]
            for b in range(bands_here):
                halos.append(halo if b == 0 else pltpu.roll(halo, LANES - 2 * ROWS * b, 1))
        block = jnp.concatenate(
            [jnp.concatenate(mains, 0), jnp.concatenate(halos, 0)], 1
        )
        turned = jnp.dot(turn, block, preferred_element_type=f32).astype(bf16)
        rows = pl.ds(pl.multiple_of(q * ROWS, ROWS), ROWS)
        for g in range(groups):
            x_main[g, rows, :] = turned[g * ROWS : (g + 1) * ROWS, :LANES]
            x_halo[g, rows, :] = turned[g * ROWS : (g + 1) * ROWS, LANES:]

    def part_copy(g, source):
        return pltpu.make_async_remote_copy(
            src_ref=mine.at[g],
            dst_ref=parts.at[source],
            send_sem=part_send.at[g],
            recv_sem=part_recv.at[source],
            device_id={"gx": g},
            device_id_type=MESH,
        )

    chunk = max(1, 256 // bands)

    @pl.loop(0, groups)
    def _(g):
        slot = g if prebuilt else 0
        if not prebuilt:
            build(g, 0)
        here, after = x_main[g], x_halo[g]
        both = jnp.zeros((2 * per_group, LANES), f32)
        upper = jnp.zeros((per_group, LANES), f32)
        for first in range(0, DELAY_TWO + WMAX, chunk):
            stacked = jnp.concatenate(
                [shifted(here, after, o) for o in range(first, first + chunk)], 0
            )
            columns = slice(first * bands, (first + chunk) * bands)
            if first < DELAY_TWO:
                both = both + jnp.dot(
                    lhs[slot, :, columns], stacked, preferred_element_type=f32
                )
            else:
                upper = upper + jnp.dot(
                    lhs[slot, 0:per_group, columns], stacked, preferred_element_type=f32
                )
        rows = pl.ds(pl.multiple_of(g * per_group, per_group), per_group)
        box_ref[rows, :] = both[:per_group] + upper
        turned = both[per_group:].T
        total = jnp.sum(turned, axis=0, keepdims=True)
        centred = turned - total / LANES
        mine[g, 0:1, 0:per_group] = total
        mine[g, 1:2, 0:per_group] = jnp.sum(centred * centred, axis=0, keepdims=True)

        @pl.when(g != me)
        def _():
            part_copy(g, me).start()

        @pl.when(g == me)
        def _():
            parts[me] = mine[g]

    def final_copy(s, source, target):
        return pltpu.make_async_remote_copy(
            src_ref=result,
            dst_ref=final.at[source],
            send_sem=final_send.at[s],
            recv_sem=final_recv.at[source],
            device_id={"gx": target},
            device_id_type=MESH,
        )

    def settle():
        @pl.loop(1, n)
        def _(s):
            part_copy(me, lax.rem(me + n - s, n)).wait_recv()

        totals = parts[:, 0, 0:per_group]
        squares = parts[:, 1, 0:per_group]
        average = jnp.sum(totals, axis=0, keepdims=True) / samples
        away = totals / LANES - average
        variance = (
            jnp.sum(squares, axis=0, keepdims=True)
            + LANES * jnp.sum(away * away, axis=0, keepdims=True)
        ) / samples
        result[0:1, 0:per_group] = own_width * average
        result[1:2, 0:per_group] = 1.0 / jnp.sqrt(own_width * (variance + 1e-05))

        @pl.loop(1, n)
        def _(s):
            final_copy(s, me, lax.rem(me + s, n)).start()

        final[me] = result[...]

        @pl.loop(1, n)
        def _(s):
            final_copy(s, me, lax.rem(me + s, n)).wait_send()

    if n > groups:
        pl.when(me < groups)(settle)
    else:
        settle()

    @pl.loop(0, groups)
    def _(g):
        @pl.when(g != me)
        def _():
            final_copy(1, g, me).wait_recv()
            part_copy(g, me).wait_send()

    res_ref[...] = final[...]

    @pl.loop(1, n)
    def _(s):
        slab_copy(s, me, lax.rem(me + s, n)).wait_send()


def norm_kernel(box_ref, res_ref, out_ref):
    groups = res_ref.shape[0]
    per_group = box_ref.shape[0] // groups
    for g in range(groups):
        rows = slice(g * per_group, (g + 1) * per_group)
        base, scale = (
            jnp.broadcast_to(res_ref[g, i : i + 1, :], (LANES, LANES)).T[:per_group]
            for i in range(2)
        )
        out_ref[rows, :] = (box_ref[rows, :] - base) * scale


def per_device(filterbank, chan_delay, sub_delay, widths):
    chan_count, samples = filterbank.shape
    groups = chan_delay.shape[0]
    n = lax.axis_size("gx")
    trials, bands = sub_delay.shape
    per_group = trials // groups
    bands_here = chan_count // SUBCH
    assert samples == n * LANES and n >= groups and chan_count == LANES
    message_rows = (bands_here + 1) * groups
    offsets = DELAY_TWO + WMAX
    slot_bytes = 2 * per_group * offsets * bands * 2
    slots = groups if groups * slot_bytes <= PREBUILD_BYTES else 1
    wide = jnp.broadcast_to(widths[:, None], (trials, LANES))
    bf16, f32 = jnp.bfloat16, jnp.float32
    vmem = pl.BlockSpec(memory_space=pltpu.VMEM)
    dma = pltpu.SemaphoreType.DMA
    boxcar, stats = pl.pallas_call(
        functools.partial(main_kernel, n),
        out_shape=(
            jax.ShapeDtypeStruct((trials, LANES), f32),
            jax.ShapeDtypeStruct((groups, 2, LANES), f32),
        ),
        in_specs=[vmem] * 4,
        out_specs=(vmem, vmem),
        scratch_shapes=[
            pltpu.VMEM((n, message_rows, LANES), bf16),
            pltpu.VMEM((n, message_rows, LANES), bf16),
            pltpu.VMEM((groups, bands, LANES), bf16),
            pltpu.VMEM((groups, bands, LANES), bf16),
            pltpu.VMEM((slots, 2 * per_group, offsets * bands), bf16),
            pltpu.VMEM((n, 2, LANES), f32),
            pltpu.VMEM((groups, 2, LANES), f32),
            pltpu.VMEM((2, LANES), f32),
            pltpu.VMEM((groups, 2, LANES), f32),
            dma((n,)),
            dma((n,)),
            dma((groups,)),
            dma((n,)),
            dma((n,)),
            dma((groups,)),
        ],
        compiler_params=pltpu.CompilerParams(
            collective_id=0, has_side_effects=True, vmem_limit_bytes=56 << 20
        ),
        name="dedisperse",
    )(filterbank, chan_delay, sub_delay, wide)
    return pl.pallas_call(
        norm_kernel,
        out_shape=jax.ShapeDtypeStruct((trials, LANES), f32),
        in_specs=[vmem] * 2,
        out_specs=vmem,
        name="normalise",
    )(boxcar, stats)


def solution(mesh):
    in_specs = (P(("beam", "gx"), None), P(None, "gx"), P(), P())
    out_specs = P("beam", "gx")
    return jax.shard_map(
        per_device, mesh=mesh, in_specs=in_specs, out_specs=out_specs, check_vma=False
    )
```

```python
import functools
import math
import jax
import jax.numpy as jnp
from jax import lax
from jax.experimental import pallas as pl
from jax.experimental.pallas import tpu as pltpu
from jax.sharding import PartitionSpec as P

SUBCH = 32
DELAY_ONE = 8
DELAY_TWO = 16
WMAX = 16
LANES = 128
ROWS = 16
PREBUILD_BYTES = 24 << 20
MESH = pl.DeviceIdType.MESH


def lane_index(rows):
    return lax.broadcasted_iota(jnp.int32, (rows, LANES), 1)


def shifted(here, after, offset):
    if offset == 0:
        return here
    mixed = jnp.where(lane_index(here.shape[0]) >= offset, here, after)
    return pltpu.roll(mixed, LANES - offset, 1)


def main_kernel(
    n,
    fb_in,
    cd_in,
    sd_in,
    w_in,
    box_ref,
    res_ref,
    fb_ref,
    cd_ref,
    sd_ref,
    w_ref,
    gaps,
    wide,
    width_rows,
    send,
    recv,
    x_main,
    x_halo,
    lhs,
    parts,
    mine,
    load_sem,
    send_sem,
    recv_sem,
    part_send,
    part_recv,
):
    me = lax.axis_index("gx")
    groups = cd_ref.shape[0]
    bands_here = cd_ref.shape[1] // SUBCH
    bands, trials = sd_ref.shape
    per_group = trials // groups
    samples = fb_ref.shape[1]
    tiles = samples // LANES
    main_rows = bands_here * groups
    rep = max(1, LANES // bands)
    width_k = rep * bands
    steps = (DELAY_TWO + WMAX) // rep
    prebuilt = lhs.shape[0] == groups
    bf16, f32 = jnp.bfloat16, jnp.float32

    barrier = pltpu.get_barrier_semaphore()

    @pl.loop(1, n)
    def _(s):
        pl.semaphore_signal(
            barrier, inc=1, device_id={"gx": lax.rem(me + s, n)}, device_id_type=MESH
        )

    loads = [
        pltpu.make_async_copy(source, target, load_sem.at[i])
        for i, (source, target) in enumerate(
            [(cd_in, cd_ref), (fb_in, fb_ref), (sd_in, sd_ref), (w_in, w_ref)]
        )
    ]
    for load in loads:
        load.start()

    loads[0].wait()
    lane = lane_index(groups)
    delays = cd_ref[...]
    code = jnp.concatenate(
        [
            jnp.where((lane >= SUBCH * b) & (lane < SUBCH * (b + 1)), delays, -1)
            for b in range(bands_here)
        ],
        0,
    )
    choose = jnp.concatenate(
        [jnp.where(code == o, 1.0, 0.0).astype(bf16) for o in range(DELAY_ONE)], 1
    )

    def tile(j):
        return fb_ref[:, pl.ds(pl.multiple_of(j * LANES, LANES), LANES)]

    def put(j, block):
        send[j, 0:main_rows, :] = block.astype(bf16)
        packed = jnp.zeros((groups, LANES), f32)
        for b in range(bands_here):
            head = jnp.where(lane < 2 * ROWS, block[b * groups : (b + 1) * groups], 0.0)
            packed = packed + (head if b == 0 else pltpu.roll(head, 2 * ROWS * b, 1))
        send[lax.rem(j + n - 1, n), main_rows : main_rows + groups, :] = packed.astype(bf16)

    loads[1].wait()

    @pl.loop(0, tiles // 2)
    def _(pair):
        first, second = tile(2 * pair), tile(2 * pair + 1)
        third = tile(jnp.minimum(2 * pair + 2, tiles - 1))
        third = jnp.where(2 * pair + 2 < tiles, third, jnp.zeros_like(third))
        stacked = jnp.concatenate(
            [
                jnp.concatenate([shifted(first, second, o), shifted(second, third, o)], 1)
                for o in range(DELAY_ONE)
            ],
            0,
        )
        block = jnp.dot(choose, stacked, preferred_element_type=f32)
        put(2 * pair, block[:, :LANES])
        put(2 * pair + 1, block[:, LANES:])

    send[n - 1, main_rows : main_rows + groups, :] = jnp.zeros((groups, LANES), bf16)

    pl.semaphore_wait(barrier, n - 1)

    def slab_copy(s, source, target):
        return pltpu.make_async_remote_copy(
            src_ref=send.at[target],
            dst_ref=recv.at[source],
            send_sem=send_sem.at[s],
            recv_sem=recv_sem.at[source],
            device_id={"gx": target},
            device_id_type=MESH,
        )

    @pl.loop(1, n)
    def _(s):
        slab_copy(s, me, lax.rem(me + s, n)).start()

    recv[me] = send[me]

    loads[2].wait()
    loads[3].wait()
    for first in range(0, trials, LANES):
        cut = slice(first, first + LANES)
        some = sd_ref[:, cut]
        gaps[cut, :] = jnp.concatenate([some - h for h in range(rep)], 0).T
        wide[cut, :] = jnp.broadcast_to(w_ref[cut].reshape(1, LANES), (LANES, LANES)).T
    for g in range(groups):
        row = wide[g * per_group : (g + 1) * per_group, :].astype(f32).T[0:1, :]
        width_rows[g : g + 1, 0:per_group] = row

    def build(g, slot):
        rows = pl.ds(pl.multiple_of(g * per_group, per_group), per_group)
        own, top = gaps[rows, :], wide[rows, :]
        if width_k > LANES:
            top = jnp.concatenate([top] * (width_k // LANES), 1)
        for p in range(steps):
            gap = p * rep - own
            columns = slice(p * width_k, (p + 1) * width_k)
            inside = jnp.where((gap >= 0) & (gap < top), 1.0, 0.0)
            lhs[slot, 0:per_group, columns] = inside.astype(bf16)
            if p * rep < DELAY_TWO:
                lhs[slot, per_group : 2 * per_group, columns] = jnp.where(
                    gap == 0, 1.0, 0.0
                ).astype(bf16)

    if prebuilt:

        @pl.loop(0, groups)
        def _(g):
            build(g, g)

    per_pack = ROWS // bands_here
    out_row = lax.broadcasted_iota(jnp.int32, (ROWS * groups, ROWS * groups), 0)
    in_row = lax.broadcasted_iota(jnp.int32, (ROWS * groups, ROWS * groups), 1)
    turn = jnp.where(
        in_row == (out_row & (ROWS - 1)) * groups + (out_row >> 4), 1.0, 0.0
    ).astype(bf16)

    @pl.loop(0, n // per_pack)
    def _(q):
        mains, halos = [], []
        for s in range(per_pack):
            source = q * per_pack + s

            @pl.when(source != me)
            def _():
                slab_copy(0, source, me).wait_recv()

            mains.append(recv[source, 0:main_rows, :])
            halo = recv[source, main_rows : main_rows + groups, :]
            for b in range(bands_here):
                halos.append(halo if b == 0 else pltpu.roll(halo, LANES - 2 * ROWS * b, 1))
        block = jnp.concatenate(
            [jnp.concatenate(mains, 0), jnp.concatenate(halos, 0)], 1
        )
        turned = jnp.dot(turn, block, preferred_element_type=f32).astype(bf16)
        rows = pl.ds(pl.multiple_of(q * ROWS, ROWS), ROWS)
        for g in range(groups):
            x_main[g, rows, :] = turned[g * ROWS : (g + 1) * ROWS, :LANES]
            x_halo[g, rows, :] = turned[g * ROWS : (g + 1) * ROWS, LANES:]

    chunk = max(1, 256 // bands)
    turns, _, _, turn_groups, _ = parts.shape

    def part_copy(c, s, source, target):
        return pltpu.make_async_remote_copy(
            src_ref=mine.at[c],
            dst_ref=parts.at[c, source],
            send_sem=part_send.at[c, s],
            recv_sem=part_recv.at[c, source],
            device_id={"gx": target},
            device_id_type=MESH,
        )

    def rows_of(g):
        return pl.ds(pl.multiple_of(g * per_group, per_group), per_group)

    def summed(g, rows, firsts):
        slot = g if prebuilt else 0
        if not prebuilt:
            build(g, 0)
        here, after = x_main[g], x_halo[g]
        total = jnp.zeros((rows, LANES), f32)
        for first in firsts:
            stacked = jnp.concatenate(
                [shifted(here, after, o) for o in range(first, first + chunk)], 0
            )
            columns = slice(first * bands, (first + chunk) * bands)
            total = total + jnp.dot(
                lhs[slot, 0:rows, columns], stacked, preferred_element_type=f32
            )
        return total

    for c in range(turns):

        @pl.loop(0, turn_groups)
        def _(r):
            g = c * turn_groups + r
            both = summed(g, 2 * per_group, range(0, DELAY_TWO, chunk))
            box_ref[rows_of(g), :] = both[:per_group]
            turned = both[per_group:].T
            total = jnp.sum(turned, axis=0, keepdims=True)
            centred = turned - total / LANES
            square = jnp.sum(centred * centred, axis=0, keepdims=True)
            mine[c, 0, pl.ds(r, 1), 0:per_group] = total
            mine[c, 1, pl.ds(r, 1), 0:per_group] = square

        @pl.loop(1, n)
        def _(s):
            part_copy(c, s, me, lax.rem(me + s, n)).start()

        parts[c, me] = mine[c]

    @pl.loop(0, groups)
    def _(g):
        upper = summed(g, per_group, range(DELAY_TWO, DELAY_TWO + WMAX, chunk))
        box_ref[rows_of(g), :] = box_ref[rows_of(g), :] + upper

    for c in range(turns):

        @pl.loop(1, n)
        def _(s):
            part_copy(c, s, lax.rem(me + n - s, n), me).wait_recv()

        cut = slice(c * turn_groups, (c + 1) * turn_groups)
        totals, squares = parts[c, :, 0], parts[c, :, 1]
        average = jnp.sum(totals, axis=0) / samples
        away = totals / LANES - average[None]
        variance = (jnp.sum(squares, axis=0) + LANES * jnp.sum(away * away, axis=0)) / samples
        width = width_rows[cut, :]
        res_ref[0, cut, :] = width * average
        res_ref[1, cut, :] = 1.0 / jnp.sqrt(width * (variance + 1e-05))

    for c in range(turns):

        @pl.loop(1, n)
        def _(s):
            part_copy(c, s, me, lax.rem(me + s, n)).wait_send()

    @pl.loop(1, n)
    def _(s):
        slab_copy(s, me, lax.rem(me + s, n)).wait_send()


def norm_kernel(box_in, res_ref, out_ref, box_ref, done, load_sems, sems):
    groups = res_ref.shape[1]
    per_group = box_ref.shape[0] // groups
    loads, copies = [], []
    for g in range(groups):
        rows = slice(g * per_group, (g + 1) * per_group)
        loads.append(pltpu.make_async_copy(box_in.at[rows], box_ref.at[rows], load_sems.at[g]))
        loads[-1].start()
    for g in range(groups):
        rows = slice(g * per_group, (g + 1) * per_group)
        base, scale = (
            jnp.broadcast_to(res_ref[i, g : g + 1, :], (LANES, LANES)).T[:per_group]
            for i in range(2)
        )
        loads[g].wait()
        done[rows, :] = (box_ref[rows, :] - base) * scale
        copies.append(pltpu.make_async_copy(done.at[rows], out_ref.at[rows], sems.at[g]))
        copies[-1].start()
    for copy in copies:
        copy.wait()


def per_device(filterbank, chan_delay, sub_delay, widths):
    chan_count, samples = filterbank.shape
    groups = chan_delay.shape[0]
    n = lax.axis_size("gx")
    trials, bands = sub_delay.shape
    per_group = trials // groups
    bands_here = chan_count // SUBCH
    assert samples == n * LANES and n >= groups and chan_count == LANES
    message_rows = (bands_here + 1) * groups
    offsets = DELAY_TWO + WMAX
    slot_bytes = 2 * per_group * offsets * bands * 2
    slots = groups if groups * slot_bytes <= PREBUILD_BYTES else 1
    turn_groups = min(8, groups)
    turns = groups // turn_groups
    rep = max(1, LANES // bands)
    bf16, f32, i32 = jnp.bfloat16, jnp.float32, jnp.int32
    arrays = [
        ((chan_count, samples), bf16),
        ((groups, chan_count), i32),
        ((bands, trials), i32),
        ((trials,), i32),
        ((trials, rep * bands), i32),
        ((trials, LANES), i32),
        ((groups, LANES), f32),
        ((n, message_rows, LANES), bf16),
        ((n, message_rows, LANES), bf16),
        ((groups, bands, LANES), bf16),
        ((groups, bands, LANES), bf16),
        ((slots, 2 * per_group, offsets * bands), bf16),
        ((turns, n, 2, turn_groups, LANES), f32),
        ((turns, 2, turn_groups, LANES), f32),
    ]
    held = sum(math.prod(shape) * jnp.dtype(kind).itemsize for shape, kind in arrays)
    vmem = pl.BlockSpec(memory_space=pltpu.VMEM)
    anywhere = pl.BlockSpec(memory_space=pl.ANY)
    dma = pltpu.SemaphoreType.DMA
    boxcar, stats = pl.pallas_call(
        functools.partial(main_kernel, n),
        out_shape=(
            jax.ShapeDtypeStruct((trials, LANES), f32),
            jax.ShapeDtypeStruct((2, groups, LANES), f32),
        ),
        in_specs=[anywhere] * 4,
        out_specs=(vmem, vmem),
        scratch_shapes=[pltpu.VMEM(shape, kind) for shape, kind in arrays]
        + [dma((4,)), dma((n,)), dma((n,)), dma((turns, n)), dma((turns, n))],
        compiler_params=pltpu.CompilerParams(
            collective_id=0, has_side_effects=True, vmem_limit_bytes=max(56 << 20, held + (10 << 20))
        ),
        name="dedisperse",
    )(filterbank, chan_delay, sub_delay.T, widths)
    return pl.pallas_call(
        norm_kernel,
        out_shape=jax.ShapeDtypeStruct((trials, LANES), f32),
        in_specs=[anywhere, vmem],
        out_specs=anywhere,
        scratch_shapes=[pltpu.VMEM((trials, LANES), f32)] * 2 + [dma((groups,))] * 2,
        compiler_params=pltpu.CompilerParams(vmem_limit_bytes=56 << 20),
        name="normalise",
    )(boxcar, stats)


def solution(mesh):
    in_specs = (P(("beam", "gx"), None), P(None, "gx"), P(), P())
    out_specs = P("beam", "gx")
    return jax.shard_map(
        per_device, mesh=mesh, in_specs=in_specs, out_specs=out_specs, check_vma=False
    )
```

```python
import functools
import math
import jax
import jax.numpy as jnp
from jax import lax
from jax.experimental import pallas as pl
from jax.experimental.pallas import tpu as pltpu
from jax.sharding import PartitionSpec as P

SUBCH = 32
DELAY_ONE = 8
DELAY_TWO = 16
WMAX = 16
LANES = 128
ROWS = 16
PREBUILD_BYTES = 24 << 20
MESH = pl.DeviceIdType.MESH


def lane_index(rows):
    return lax.broadcasted_iota(jnp.int32, (rows, LANES), 1)


def shifted(here, after, offset):
    if offset == 0:
        return here
    mixed = jnp.where(lane_index(here.shape[0]) >= offset, here, after)
    return pltpu.roll(mixed, LANES - offset, 1)


def main_kernel(
    n,
    fb_in,
    cd_in,
    sd_in,
    w_in,
    box_ref,
    fb_ref,
    cd_ref,
    sd_ref,
    w_ref,
    gaps,
    wide,
    width_rows,
    send,
    recv,
    x_main,
    x_halo,
    lhs,
    parts,
    mine,
    res_ref,
    load_sem,
    send_sem,
    recv_sem,
    part_send,
    part_recv,
):
    me = lax.axis_index("gx")
    groups = cd_ref.shape[0]
    bands_here = cd_ref.shape[1] // SUBCH
    bands, trials = sd_ref.shape
    per_group = trials // groups
    samples = fb_ref.shape[1]
    tiles = samples // LANES
    main_rows = bands_here * groups
    rep = max(1, LANES // bands)
    width_k = rep * bands
    steps = (DELAY_TWO + WMAX) // rep
    prebuilt = lhs.shape[0] == groups
    bf16, f32 = jnp.bfloat16, jnp.float32

    barrier = pltpu.get_barrier_semaphore()

    @pl.loop(1, n)
    def _(s):
        pl.semaphore_signal(
            barrier, inc=1, device_id={"gx": lax.rem(me + s, n)}, device_id_type=MESH
        )

    loads = [
        pltpu.make_async_copy(source, target, load_sem.at[i])
        for i, (source, target) in enumerate(
            [(cd_in, cd_ref), (fb_in, fb_ref), (sd_in, sd_ref), (w_in, w_ref)]
        )
    ]
    for load in loads:
        load.start()

    loads[0].wait()
    lane = lane_index(groups)
    delays = cd_ref[...]
    code = jnp.concatenate(
        [
            jnp.where((lane >= SUBCH * b) & (lane < SUBCH * (b + 1)), delays, -1)
            for b in range(bands_here)
        ],
        0,
    )
    choose = jnp.concatenate(
        [jnp.where(code == o, 1.0, 0.0).astype(bf16) for o in range(DELAY_ONE)], 1
    )

    def tile(j):
        return fb_ref[:, pl.ds(pl.multiple_of(j * LANES, LANES), LANES)]

    def put(j, block):
        send[j, 0:main_rows, :] = block.astype(bf16)
        packed = jnp.zeros((groups, LANES), f32)
        for b in range(bands_here):
            head = jnp.where(lane < 2 * ROWS, block[b * groups : (b + 1) * groups], 0.0)
            packed = packed + (head if b == 0 else pltpu.roll(head, 2 * ROWS * b, 1))
        send[lax.rem(j + n - 1, n), main_rows : main_rows + groups, :] = packed.astype(bf16)

    loads[1].wait()

    @pl.loop(0, tiles // 2, unroll=4)
    def _(pair):
        first, second = tile(2 * pair), tile(2 * pair + 1)
        third = tile(jnp.minimum(2 * pair + 2, tiles - 1))
        third = jnp.where(2 * pair + 2 < tiles, third, jnp.zeros_like(third))
        stacked = jnp.concatenate(
            [
                jnp.concatenate([shifted(first, second, o), shifted(second, third, o)], 1)
                for o in range(DELAY_ONE)
            ],
            0,
        )
        block = jnp.dot(choose, stacked, preferred_element_type=f32)
        put(2 * pair, block[:, :LANES])
        put(2 * pair + 1, block[:, LANES:])

    send[n - 1, main_rows : main_rows + groups, :] = jnp.zeros((groups, LANES), bf16)

    pl.semaphore_wait(barrier, n - 1)

    def slab_copy(s, source, target):
        return pltpu.make_async_remote_copy(
            src_ref=send.at[target],
            dst_ref=recv.at[source],
            send_sem=send_sem.at[s],
            recv_sem=recv_sem.at[source],
            device_id={"gx": target},
            device_id_type=MESH,
        )

    @pl.loop(1, n)
    def _(s):
        slab_copy(s, me, lax.rem(me + s, n)).start()

    recv[me] = send[me]

    loads[2].wait()
    loads[3].wait()
    for first in range(0, trials, LANES):
        cut = slice(first, first + LANES)
        some = sd_ref[:, cut]
        gaps[cut, :] = jnp.concatenate([some - h for h in range(rep)], 0).T
        wide[cut, :] = jnp.broadcast_to(w_ref[cut].reshape(1, LANES), (LANES, LANES)).T
    for g in range(groups):
        row = wide[g * per_group : (g + 1) * per_group, :].astype(f32).T[0:1, :]
        width_rows[g : g + 1, 0:per_group] = row

    def build(g, slot):
        rows = pl.ds(pl.multiple_of(g * per_group, per_group), per_group)
        own, top = gaps[rows, :], wide[rows, :]
        if width_k > LANES:
            top = jnp.concatenate([top] * (width_k // LANES), 1)
        for p in range(steps):
            gap = p * rep - own
            columns = slice(p * width_k, (p + 1) * width_k)
            inside = jnp.where((gap >= 0) & (gap < top), 1.0, 0.0)
            lhs[slot, 0:per_group, columns] = inside.astype(bf16)
            if p * rep < DELAY_TWO:
                lhs[slot, per_group : 2 * per_group, columns] = jnp.where(
                    gap == 0, 1.0, 0.0
                ).astype(bf16)

    if prebuilt:

        @pl.loop(0, groups)
        def _(g):
            build(g, g)

    per_pack = ROWS // bands_here
    out_row = lax.broadcasted_iota(jnp.int32, (ROWS * groups, ROWS * groups), 0)
    in_row = lax.broadcasted_iota(jnp.int32, (ROWS * groups, ROWS * groups), 1)
    turn = jnp.where(
        in_row == (out_row & (ROWS - 1)) * groups + (out_row >> 4), 1.0, 0.0
    ).astype(bf16)

    @pl.loop(0, n // per_pack, unroll=4)
    def _(q):
        mains, halos = [], []
        for s in range(per_pack):
            source = q * per_pack + s

            @pl.when(source != me)
            def _():
                slab_copy(0, source, me).wait_recv()

            mains.append(recv[source, 0:main_rows, :])
            halo = recv[source, main_rows : main_rows + groups, :]
            for b in range(bands_here):
                halos.append(halo if b == 0 else pltpu.roll(halo, LANES - 2 * ROWS * b, 1))
        block = jnp.concatenate(
            [jnp.concatenate(mains, 0), jnp.concatenate(halos, 0)], 1
        )
        turned = jnp.dot(turn, block, preferred_element_type=f32).astype(bf16)
        rows = pl.ds(pl.multiple_of(q * ROWS, ROWS), ROWS)
        for g in range(groups):
            x_main[g, rows, :] = turned[g * ROWS : (g + 1) * ROWS, :LANES]
            x_halo[g, rows, :] = turned[g * ROWS : (g + 1) * ROWS, LANES:]

    chunk = max(1, 256 // bands)
    turns, _, _, turn_groups, _ = parts.shape

    def part_copy(c, s, source, target):
        return pltpu.make_async_remote_copy(
            src_ref=mine.at[c],
            dst_ref=parts.at[c, source],
            send_sem=part_send.at[c, s],
            recv_sem=part_recv.at[c, source],
            device_id={"gx": target},
            device_id_type=MESH,
        )

    def rows_of(g):
        return pl.ds(pl.multiple_of(g * per_group, per_group), per_group)

    def summed(g, rows, firsts):
        slot = g if prebuilt else 0
        if not prebuilt:
            build(g, 0)
        here, after = x_main[g], x_halo[g]
        total = jnp.zeros((rows, LANES), f32)
        for first in firsts:
            stacked = jnp.concatenate(
                [shifted(here, after, o) for o in range(first, first + chunk)], 0
            )
            columns = slice(first * bands, (first + chunk) * bands)
            total = total + jnp.dot(
                lhs[slot, 0:rows, columns], stacked, preferred_element_type=f32
            )
        return total

    for c in range(turns):

        @pl.loop(0, turn_groups, unroll=8)
        def _(r):
            g = c * turn_groups + r
            both = summed(g, 2 * per_group, range(0, DELAY_TWO, chunk))
            box_ref[rows_of(g), :] = both[:per_group]
            turned = both[per_group:].T
            total = jnp.sum(turned, axis=0, keepdims=True)
            centred = turned - total / LANES
            square = jnp.sum(centred * centred, axis=0, keepdims=True)
            mine[c, 0, pl.ds(r, 1), 0:per_group] = total
            mine[c, 1, pl.ds(r, 1), 0:per_group] = square

        @pl.loop(1, n)
        def _(s):
            part_copy(c, s, me, lax.rem(me + s, n)).start()

        parts[c, me] = mine[c]

    @pl.loop(0, groups, unroll=8)
    def _(g):
        upper = summed(g, per_group, range(DELAY_TWO, DELAY_TWO + WMAX, chunk))
        box_ref[rows_of(g), :] = box_ref[rows_of(g), :] + upper

    for c in range(turns):

        @pl.loop(1, n)
        def _(s):
            part_copy(c, s, lax.rem(me + n - s, n), me).wait_recv()

        cut = slice(c * turn_groups, (c + 1) * turn_groups)
        totals, squares = parts[c, :, 0], parts[c, :, 1]
        average = jnp.sum(totals, axis=0) / samples
        away = totals / LANES - average[None]
        variance = (jnp.sum(squares, axis=0) + LANES * jnp.sum(away * away, axis=0)) / samples
        width = width_rows[cut, :]
        res_ref[0, cut, :] = width * average
        res_ref[1, cut, :] = 1.0 / jnp.sqrt(width * (variance + 1e-05))

    @pl.loop(0, groups // 4)
    def _(q):
        for r in range(4):
            g = q * 4 + r
            rows = rows_of(g)
            base, scale = (
                jnp.broadcast_to(res_ref[i, pl.ds(g, 1), :], (LANES, LANES)).T[:per_group]
                for i in range(2)
            )
            box_ref[rows, :] = (box_ref[rows, :] - base) * scale

    for c in range(turns):

        @pl.loop(1, n)
        def _(s):
            part_copy(c, s, me, lax.rem(me + s, n)).wait_send()

    @pl.loop(1, n)
    def _(s):
        slab_copy(s, me, lax.rem(me + s, n)).wait_send()


def per_device(filterbank, chan_delay, sub_delay, widths):
    chan_count, samples = filterbank.shape
    groups = chan_delay.shape[0]
    n = lax.axis_size("gx")
    trials, bands = sub_delay.shape
    per_group = trials // groups
    bands_here = chan_count // SUBCH
    assert samples == n * LANES and n >= groups and chan_count == LANES
    message_rows = (bands_here + 1) * groups
    offsets = DELAY_TWO + WMAX
    slot_bytes = 2 * per_group * offsets * bands * 2
    slots = groups if groups * slot_bytes <= PREBUILD_BYTES else 1
    turn_groups = min(8, groups)
    turns = groups // turn_groups
    rep = max(1, LANES // bands)
    bf16, f32, i32 = jnp.bfloat16, jnp.float32, jnp.int32
    arrays = [
        ((chan_count, samples), bf16),
        ((groups, chan_count), i32),
        ((bands, trials), i32),
        ((trials,), i32),
        ((trials, rep * bands), i32),
        ((trials, LANES), i32),
        ((groups, LANES), f32),
        ((n, message_rows, LANES), bf16),
        ((n, message_rows, LANES), bf16),
        ((groups, bands, LANES), bf16),
        ((groups, bands, LANES), bf16),
        ((slots, 2 * per_group, offsets * bands), bf16),
        ((turns, n, 2, turn_groups, LANES), f32),
        ((turns, 2, turn_groups, LANES), f32),
        ((2, groups, LANES), f32),
    ]
    held = sum(math.prod(shape) * jnp.dtype(kind).itemsize for shape, kind in arrays)
    vmem = pl.BlockSpec(memory_space=pltpu.VMEM)
    anywhere = pl.BlockSpec(memory_space=pl.ANY)
    dma = pltpu.SemaphoreType.DMA
    return pl.pallas_call(
        functools.partial(main_kernel, n),
        out_shape=jax.ShapeDtypeStruct((trials, LANES), f32),
        in_specs=[anywhere] * 4,
        out_specs=vmem,
        scratch_shapes=[pltpu.VMEM(shape, kind) for shape, kind in arrays]
        + [dma((4,)), dma((n,)), dma((n,)), dma((turns, n)), dma((turns, n))],
        compiler_params=pltpu.CompilerParams(
            collective_id=0, has_side_effects=True, vmem_limit_bytes=max(56 << 20, held + (10 << 20))
        ),
        name="dedisperse",
    )(filterbank, chan_delay, sub_delay.T, widths)

def solution(mesh):
    in_specs = (P(("beam", "gx"), None), P(None, "gx"), P(), P())
    out_specs = P("beam", "gx")
    return jax.shard_map(
        per_device, mesh=mesh, in_specs=in_specs, out_specs=out_specs, check_vma=False
    )
```
